256 devices in a mesh: rep: 16 (over x, z_hi, core), fsdp: 16 (over y, z_lo).
Axes of the slice: x: 4, y: 4, z: 8 (z_hi: 2, z_lo: 4; z = z_hi * 4 + z_lo), core: 2. Of those that a mesh axis runs over, the one named last changes fastest.
Arguments:
- inputs: bfloat16 [16, 8192, 8192], P('rep', 'fsdp'), may hold values from -6 to 6
- targets: bfloat16 [16, 8192, 512], P('rep', 'fsdp'), may hold values from -3 to 3
- replica_drift: bfloat16 [16, 8192, 512], P('rep', 'fsdp'), may hold values from -0.359375 to 0.359375
- first_moment: float32 [16, 8192, 512], P('rep', 'fsdp'), may hold values from -3.6621095e-05 to 3.6621095e-05
- second_moment: float32 [16, 8192, 512], P('rep', 'fsdp'), may hold values from 2.9802324e-11 to 7.4505807e-10
- base_weight: float32 [8192, 512], P('fsdp'), may hold values from -6 to 6
- momentum: float32 [8192, 512], P('fsdp'), may hold values from -0.6 to 0.6
Outputs:
- new_base: float32 [8192, 512], P('fsdp')
- new_momentum: float32 [8192, 512], P('fsdp')
The draws below stay inside these ranges and needn't reach their ends.
All inputs are finite; a program needn't handle non-finite values.
Results may differ from the reference program's by a relative error of at most 0.012.
Values may be sent and summed in bfloat16 or wider, within the bound.
No kernel may reach another device: no remote copies, remote signals or barrier semaphores. Data moves between devices by JAX's collectives and lax.ppermute only.
A program may use at most 128 MiB of HBM per device.

```python
import math
import jax
import jax.numpy as jnp
from jax import lax

D = 8192
C = 512
TOK_DEV = 512
TOKENS = 8192
REPS = 16
N_FSDP = 16


def levels(own_key, shape, cuts, low, largest):
    gain, own = 1.0, jax.random.fold_in(own_key, 6)
    for position, shards_of in cuts:
        steps = jnp.exp(jax.random.uniform(jax.random.fold_in(own, position), (shards_of,), jnp.float32, low / len(cuts), largest / len(cuts)))
        gain = gain * jnp.repeat(steps, shape[position] // shards_of).reshape([-1 if axis == position else 1 for axis in range(len(shape))])
    return gain


def normal_values(own_key, shape, scale, reach, shards=(), held_as=jnp.bfloat16):
    factor_of = levels(own_key, shape, shards, -0.22, 0.18) if shards else 1.0
    values = jax.random.normal(own_key, shape, jnp.float32) * scale * factor_of
    return jnp.minimum(jnp.maximum(values, -reach), reach).astype(held_as)


def setup_inputs(seed: int = 0) -> dict:
    key_list = jax.random.split(jax.random.key(seed), 8)
    return {
        "inputs": normal_values(key_list[0], (REPS, TOKENS, D), 1.0, 6.0, ((0, 16), (1, 16))),
        "targets": normal_values(key_list[1], (REPS, TOKENS, C), 0.5, 3.0, ((0, 16), (1, 16))),
        "replica_drift": normal_values(key_list[2], (REPS, D, C), 0.06, 0.359375, ((0, 16), (1, 16))),
        "first_moment": normal_values(key_list[3], (REPS, D, C), (0.05 / (D * TOKENS) ** 0.5), 3.662109520519152e-05, ((0, 16), (1, 16)), jnp.float32),
        "second_moment": jnp.clip(jnp.exp(math.log(7.450580707946131e-10) - 3.218876 * jax.random.uniform(key_list[4], (REPS, D, C), jnp.float32) ** levels(key_list[4], (REPS, D, C), ((0, 16), (1, 16)), -0.2, 0.2)), 2.980232380322967e-11, 7.450580707946131e-10),
        "base_weight": normal_values(key_list[5], (D, C), 1.0, 6.0, ((0, 16),), jnp.float32),
        "momentum": normal_values(key_list[6], (D, C), 0.1, 0.6, ((0, 16),), jnp.float32),
    }


LEARN_RATE = 1.0
BETA_ONE = 0.9
BETA_TWO = 0.95
ADAM_EPS = 1e-08
DECAY = 0.1
OUTER_MU = 0.9
OUTER_RATE = 0.7

def replica_codes(inputs_one, targets_one, drift_one, first_one, second_one, base_weight):
    local_weight = base_weight + drift_one.astype(jnp.float32)
    low_weight = local_weight.astype(jnp.bfloat16)
    projected = jnp.dot(inputs_one, low_weight, preferred_element_type=jnp.float32) / jnp.sqrt(jnp.float32(D))
    residual_rows = (projected - targets_one.astype(jnp.float32)).astype(jnp.bfloat16)
    grad_scale = 1.0 / (jnp.sqrt(jnp.float32(D)) * jnp.float32(TOKENS))
    groups_in = inputs_one.reshape(N_FSDP, TOK_DEV, D)
    groups_res = residual_rows.reshape(N_FSDP, TOK_DEV, C)

    def add_group(total, pair):
        term = lax.dot_general(pair[0], pair[1], (((0,), (0,)), ((), ())), preferred_element_type=jnp.float32) * grad_scale
        rounded = lax.optimization_barrier(term.astype(jnp.bfloat16))
        return (total + rounded.astype(jnp.float32), None)
    gradient, unused = lax.scan(add_group, jnp.zeros((D, C), jnp.float32), (groups_in, groups_res))
    moment_one = BETA_ONE * first_one + (1.0 - BETA_ONE) * gradient
    moment_two = BETA_TWO * second_one + (1.0 - BETA_TWO) * gradient * gradient
    update_delta = LEARN_RATE * (moment_one / (jnp.sqrt(moment_two) + ADAM_EPS) + DECAY * local_weight) - drift_one.astype(jnp.float32)
    codes = lax.optimization_barrier(update_delta.astype(jnp.bfloat16))
    return codes.astype(jnp.float32)

def reference(inputs, targets, replica_drift, first_moment, second_moment, base_weight, momentum):

    def add_replica(total, items):
        widened = replica_codes(items[0], items[1], items[2], items[3], items[4], base_weight)
        return (total + widened, None)
    total, unused = lax.scan(add_replica, jnp.zeros((D, C), jnp.float32), (inputs, targets, replica_drift, first_moment, second_moment))
    mean_delta = total / jnp.float32(REPS)
    new_momentum = OUTER_MU * momentum + mean_delta
    new_base = base_weight - OUTER_RATE * (mean_delta + OUTER_MU * new_momentum)
    return (new_base, new_momentum)
```

```python
import jax
import jax.numpy as jnp
from jax import lax
from jax.sharding import PartitionSpec as P

LEARN_RATE = 1.0
BETA_ONE = 0.9
BETA_TWO = 0.95
ADAM_EPS = 1e-08
DECAY = 0.1
OUTER_MU = 0.9
OUTER_RATE = 0.7

NY, NZ = 4, 4
BF, F32 = jnp.bfloat16, jnp.float32


def y_shift(dy):
    return [(y * NZ + z, ((y + dy) % NY) * NZ + z) for y in range(NY) for z in range(NZ)]


def z_pairs(pairs):
    return [(y * NZ + a, y * NZ + b) for y in range(NY) for a, b in pairs]


UP, DOWN = y_shift(1), y_shift(-1)
SWAP = z_pairs([(0, 1), (1, 0), (2, 3), (3, 2)])
MIDDLE = z_pairs([(1, 2), (2, 1)])
OUTWARD = z_pairs([(1, 0), (2, 3)])
INWARD = z_pairs([(0, 1), (3, 2)])


def rep_shift(dx, dh, dc):
    return [
        ((x * 2 + h) * 2 + c, (((x + dx) % 4) * 2 + (h ^ dh)) * 2 + (c ^ dc))
        for x in range(4)
        for h in range(2)
        for c in range(2)
    ]


def send(value, pairs):
    return lax.ppermute(value, "fsdp", pairs)


def send_rep(value, dx, dh, dc):
    return lax.ppermute(value, "rep", rep_shift(dx, dh, dc))


def gather_columns(own, z):
    inner = (z == 1) | (z == 2)
    pair = send(own, SWAP)
    mid_one = send(own, MIDDLE)
    mid_two = send(pair, MIDDLE)
    far_one = jnp.where(inner, mid_one, send(mid_one, OUTWARD))
    far_two = jnp.where(inner, mid_two, send(mid_two, OUTWARD))
    return [own, pair, far_one, far_two]


def column_ids(z):
    return [z, z ^ 1, jnp.where(z < 2, 2, 1), jnp.where(z < 2, 3, 0)]


def gather_ring(block):
    half = block.shape[0] // 2
    below = send(block, UP)
    above = send(block, DOWN)
    far_top = send(below[:half], UP)
    far_bottom = send(above[half:], DOWN)
    return block, below, above, far_top, far_bottom


def reduce_ring(own, upper, lower, far):
    half = far.shape[0] // 2
    top = send(far[:half], UP)
    bottom = send(far[half:], DOWN)
    upper = jnp.concatenate([(upper[:half].astype(F32) + top.astype(F32)).astype(BF), upper[half:]], 0)
    lower = jnp.concatenate([lower[:half], (lower[half:].astype(F32) + bottom.astype(F32)).astype(BF)], 0)
    return own.astype(F32) + send(upper, UP).astype(F32) + send(lower, DOWN).astype(F32)


def reduce_rep(codes):
    rep = lax.axis_index("rep")
    x, core = rep // 4, rep % 2
    rows = codes.shape[0]
    half, piece = rows // 2, rows // 8
    mine = lax.dynamic_slice_in_dim(codes, core * half, half, 0)
    other = lax.dynamic_slice_in_dim(codes, (1 - core) * half, half, 0)
    pair = mine.astype(F32) + send_rep(other, 0, 0, 1).astype(F32)
    part = lambda d: lax.dynamic_slice_in_dim(pair, ((x + d) % 4) * piece, piece, 0)
    total = part(0)
    for d in (1, 2, 3):
        total = total + send_rep(part(d).astype(BF), d, 0, 0).astype(F32)
    rounded = total.astype(BF)
    total = rounded.astype(F32) + send_rep(rounded, 0, 1, 0).astype(F32)
    pieces = jnp.zeros((half, codes.shape[1]), F32)
    pieces = lax.dynamic_update_slice_in_dim(pieces, total, x * piece, 0)
    for d in (1, 2, 3):
        pieces = lax.dynamic_update_slice_in_dim(
            pieces, send_rep(total, d, 0, 0), ((x - d) % 4) * piece, 0
        )
    theirs = send_rep(pieces, 0, 0, 1)
    low = jnp.where(core == 0, pieces, theirs)
    high = jnp.where(core == 0, theirs, pieces)
    return jnp.concatenate([low, high], 0)


def outer_step(mean_delta, momentum, base_weight):
    new_momentum = OUTER_MU * momentum + mean_delta
    new_base = base_weight - OUTER_RATE * (mean_delta + OUTER_MU * new_momentum)
    return (new_base, new_momentum)


def on_device(inputs, targets, replica_drift, first_moment, second_moment, base_weight, momentum):
    tok_rows = inputs[0]
    width = tok_rows.shape[1]
    shard_rows = base_weight.shape[0]
    index = lax.axis_index("fsdp")
    y, z = index // NZ, index % NZ
    drift_local = replica_drift[0].astype(F32)
    local_weight = base_weight + drift_local
    low_weight = local_weight.astype(BF)

    def tokens(row, column, begin, size):
        start = (row % NY * NZ + column) * shard_rows + begin
        return lax.dynamic_slice_in_dim(tok_rows, start, size, 1)

    half = shard_rows // 2
    projected = jnp.zeros((tok_rows.shape[0], low_weight.shape[1]), F32)
    for block, column in zip(gather_columns(low_weight, z), column_ids(z)):
        same, below, above, far_top, far_bottom = gather_ring(block)
        for row, begin, part in (
            (y, 0, same),
            (y - 1, 0, below),
            (y + 1, 0, above),
            (y + 2, 0, far_top),
            (y + 2, half, far_bottom),
        ):
            projected += jnp.dot(
                tokens(row, column, begin, part.shape[0]), part, preferred_element_type=F32
            )
    projected = projected / jnp.sqrt(F32(width))
    residual_rows = (projected - targets[0].astype(F32)).astype(BF)
    all_tokens = tok_rows.shape[0] * lax.axis_size("fsdp")
    grad_scale = 1.0 / (jnp.sqrt(F32(width)) * F32(all_tokens))

    def term(row, column):
        product = lax.dot_general(
            tokens(row, column, 0, shard_rows),
            residual_rows,
            (((0,), (0,)), ((), ())),
            preferred_element_type=F32,
        )
        return (product * grad_scale).astype(BF)

    def column_sum(column):
        return reduce_ring(term(y, column), term(y + 1, column), term(y - 1, column), term(y + 2, column))

    ids = column_ids(z)
    far_two = column_sum(ids[3])
    far_two = far_two + send(far_two.astype(BF), INWARD).astype(F32)
    far_one = column_sum(ids[2])
    far_one = far_one + send(far_one.astype(BF), INWARD).astype(F32)
    pair = column_sum(ids[1]) + send(far_two.astype(BF), MIDDLE).astype(F32)
    gradient = (
        column_sum(ids[0])
        + send(far_one.astype(BF), MIDDLE).astype(F32)
        + send(pair.astype(BF), SWAP).astype(F32)
    )

    moment_one = BETA_ONE * first_moment[0] + (1.0 - BETA_ONE) * gradient
    moment_two = BETA_TWO * second_moment[0] + (1.0 - BETA_TWO) * gradient * gradient
    update_delta = (
        LEARN_RATE * (moment_one / (jnp.sqrt(moment_two) + ADAM_EPS) + DECAY * local_weight)
        - drift_local
    )
    codes = update_delta.astype(BF)
    mean_delta = reduce_rep(codes) / F32(lax.axis_size("rep"))
    return outer_step(mean_delta, momentum, base_weight)


def solution(mesh):
    placed = (
        P("rep", "fsdp", None),
        P("rep", "fsdp", None),
        P("rep", "fsdp", None),
        P("rep", "fsdp", None),
        P("rep", "fsdp", None),
        P("fsdp", None),
        P("fsdp", None),
    )
    return jax.shard_map(
        on_device,
        mesh=mesh,
        in_specs=placed,
        out_specs=(P("fsdp", None), P("fsdp", None)),
        check_vma=False,
    )
```

```python
import functools

import jax
import jax.numpy as jnp
from jax import lax
from jax.sharding import PartitionSpec as P

LEARN_RATE = 1.0
BETA_ONE = 0.9
BETA_TWO = 0.95
ADAM_EPS = 1e-08
DECAY = 0.1
OUTER_MU = 0.9
OUTER_RATE = 0.7

NY, NZ = 4, 4
BF, F32 = jnp.bfloat16, jnp.float32


def y_shift(dy):
    return [(y * NZ + z, ((y + dy) % NY) * NZ + z) for y in range(NY) for z in range(NZ)]


def z_pairs(pairs):
    return [(y * NZ + a, y * NZ + b) for y in range(NY) for a, b in pairs]


UP, DOWN = y_shift(1), y_shift(-1)
SWAP = z_pairs([(0, 1), (1, 0), (2, 3), (3, 2)])
MIDDLE = z_pairs([(1, 2), (2, 1)])
OUTWARD = z_pairs([(1, 0), (2, 3)])
INWARD = z_pairs([(0, 1), (3, 2)])


def rep_shift(dx, dh, dc):
    return [
        ((x * 2 + h) * 2 + c, (((x + dx) % 4) * 2 + (h ^ dh)) * 2 + (c ^ dc))
        for x in range(4)
        for h in range(2)
        for c in range(2)
    ]


send = functools.partial(lax.ppermute, axis_name="fsdp")


def send_rep(value, dx, dh, dc):
    return lax.ppermute(value, "rep", rep_shift(dx, dh, dc))


def after(value, *earlier):
    rows = sum(array[:1].astype(F32) for array in earlier)
    return jnp.where(rows == rows, value, jnp.zeros_like(value))


def column_ids(z):
    return z, z ^ 1, jnp.where(z < 2, 2, 1), jnp.where(z < 2, 3, 0)


def reduce_rep(codes):
    rep = lax.axis_index("rep")
    x, core = rep // 4, rep % 2
    rows = codes.shape[0]
    half, piece = rows // 2, rows // 8
    mine = lax.dynamic_slice_in_dim(codes, core * half, half, 0)
    other = lax.dynamic_slice_in_dim(codes, (1 - core) * half, half, 0)
    pair = mine.astype(F32) + send_rep(other, 0, 0, 1).astype(F32)
    part = lambda d: lax.dynamic_slice_in_dim(pair, ((x + d) % 4) * piece, piece, 0)
    total = part(0)
    for d in (1, 2, 3):
        total = total + send_rep(part(d).astype(BF), d, 0, 0).astype(F32)
    rounded = total.astype(BF)
    total = rounded.astype(F32) + send_rep(rounded, 0, 1, 0).astype(F32)
    pieces = jnp.zeros((half, codes.shape[1]), F32)
    pieces = lax.dynamic_update_slice_in_dim(pieces, total, x * piece, 0)
    for d in (1, 2, 3):
        pieces = lax.dynamic_update_slice_in_dim(
            pieces, send_rep(total, d, 0, 0), ((x - d) % 4) * piece, 0
        )
    theirs = send_rep(pieces, 0, 0, 1)
    low = jnp.where(core == 0, pieces, theirs)
    high = jnp.where(core == 0, theirs, pieces)
    return jnp.concatenate([low, high], 0)


def outer_step(mean_delta, momentum, base_weight):
    new_momentum = OUTER_MU * momentum + mean_delta
    new_base = base_weight - OUTER_RATE * (mean_delta + OUTER_MU * new_momentum)
    return (new_base, new_momentum)


def on_device(inputs, targets, replica_drift, first_moment, second_moment, base_weight, momentum):
    tok_rows = inputs[0]
    width = tok_rows.shape[1]
    shard_rows = base_weight.shape[0]
    index = lax.axis_index("fsdp")
    y, z = index // NZ, index % NZ
    drift_local = replica_drift[0].astype(F32)
    local_weight = base_weight + drift_local
    low_weight = local_weight.astype(BF)

    def tokens(row, column, begin, size):
        start = ((y + row) % NY * NZ + column) * shard_rows + begin
        return lax.dynamic_slice_in_dim(tok_rows, start, size, 1)

    half = shard_rows // 2
    own_id, pair_id, near_id, far_id = column_ids(z)
    inner = (z == 1) | (z == 2)

    def add(total, row, column, part, begin=0):
        return total + jnp.dot(
            tokens(row, column, begin, part.shape[0]), part, preferred_element_type=F32
        )

    own = low_weight
    pair = send(own, perm=SWAP)
    near_in = send(own, perm=MIDDLE)
    own_below = send(own, perm=UP)
    own_above = send(own, perm=DOWN)
    far_in = send(pair, perm=MIDDLE)
    near_out = send(near_in, perm=OUTWARD)
    pair_below = send(pair, perm=UP)
    pair_above = send(pair, perm=DOWN)
    own_top = send(own_below[:half], perm=UP)
    own_bottom = send(own_above[half:], perm=DOWN)
    far_out = send(far_in, perm=OUTWARD)
    near = after(jnp.where(inner, near_in, near_out), pair_below, pair_above)
    near_below = send(near, perm=UP)
    near_above = send(near, perm=DOWN)

    total = jnp.dot(tokens(0, own_id, 0, shard_rows), own, preferred_element_type=F32)
    total = after(add(total, 0, pair_id, pair), near_out)
    total = add(total, -1, own_id, own_below)
    total = after(add(total, 1, own_id, own_above), near_out)

    pair_top = send(after(pair_below[:half], own_top, own_bottom), perm=UP)
    pair_bottom = send(after(pair_above[half:], own_top, own_bottom), perm=DOWN)
    far = after(jnp.where(inner, far_in, far_out), near_below, near_above, total)
    far_below = send(far, perm=UP)
    far_above = send(far, perm=DOWN)

    total = add(total, 2, own_id, own_top, 0)
    total = add(total, 2, own_id, own_bottom, half)
    total = add(total, -1, pair_id, pair_below)
    total = add(total, 1, pair_id, pair_above)
    total = add(total, 0, near_id, near)
    total = add(total, -1, near_id, near_below)
    total = add(total, 1, near_id, near_above)

    near_top = send(after(near_below[:half], pair_top, pair_bottom, total), perm=UP)
    near_bottom = send(after(near_above[half:], pair_top, pair_bottom, total), perm=DOWN)
    total = add(total, 2, pair_id, pair_top, 0)
    total = add(total, 2, pair_id, pair_bottom, half)
    total = add(total, 0, far_id, far)
    far_top = send(after(far_below[:half], total), perm=UP)
    far_bottom = send(after(far_above[half:], total), perm=DOWN)
    total = add(total, -1, far_id, far_below)
    total = add(total, 1, far_id, far_above)
    total = add(total, 2, near_id, near_top, 0)
    total = add(total, 2, near_id, near_bottom, half)
    total = add(total, 2, far_id, far_top, 0)
    total = add(total, 2, far_id, far_bottom, half)

    projected = total / jnp.sqrt(F32(width))
    residual_rows = (projected - targets[0].astype(F32)).astype(BF)
    all_tokens = tok_rows.shape[0] * lax.axis_size("fsdp")
    grad_scale = 1.0 / (jnp.sqrt(F32(width)) * F32(all_tokens))

    def term(row, column, begin=0, size=shard_rows):
        product = lax.dot_general(
            tokens(row, column, begin, size),
            residual_rows,
            (((0,), (0,)), ((), ())),
            preferred_element_type=F32,
        )
        return (product * grad_scale).astype(BF)

    def plus(first, *others):
        return sum((other.astype(F32) for other in others), first.astype(F32))

    def upper(block, top):
        return jnp.concatenate([plus(block[:half], top).astype(BF), block[half:]], 0)

    def lower(block, bottom):
        return jnp.concatenate([block[:half], plus(block[half:], bottom).astype(BF)], 0)

    far_top = send(term(2, far_id, 0, half), perm=UP)
    far_bottom = send(term(2, far_id, half, half), perm=DOWN)
    near_top = send(term(2, near_id, 0, half), perm=UP)
    near_bottom = send(term(2, near_id, half, half), perm=DOWN)
    far_up = send(upper(term(1, far_id), far_top), perm=UP)
    far_down = send(lower(term(-1, far_id), far_bottom), perm=DOWN)
    gate = (far_top, far_bottom)
    near_up_term = after(term(1, near_id), *gate)
    near_down_term = after(term(-1, near_id), *gate)
    far_term = after(term(0, far_id), *gate)
    gate = (near_top, near_bottom)
    pair_top = send(after(term(2, pair_id, 0, half), *gate), perm=UP)
    pair_bottom = send(after(term(2, pair_id, half, half), *gate), perm=DOWN)
    gate = (far_up, far_down)
    far_sum = plus(far_term, far_up, far_down)
    far_in = send(far_sum.astype(BF), perm=INWARD)
    near_up = send(after(upper(near_up_term, near_top), *gate), perm=UP)
    near_down = send(after(lower(near_down_term, near_bottom), *gate), perm=DOWN)
    own_top = send(after(term(2, own_id, 0, half), *gate), perm=UP)
    own_bottom = send(after(term(2, own_id, half, half), *gate), perm=DOWN)
    near_term = after(term(0, near_id), *gate)
    pair_up_term = after(term(1, pair_id), *gate)
    pair_down_term = after(term(-1, pair_id), *gate)
    gate = (own_top, own_bottom)
    pair_up = send(after(upper(pair_up_term, pair_top), *gate), perm=UP)
    pair_down = send(after(lower(pair_down_term, pair_bottom), *gate), perm=DOWN)
    far_mid = send(plus(far_sum, far_in).astype(BF), perm=MIDDLE)
    near_sum = plus(near_term, near_up, near_down)
    near_in = send(near_sum.astype(BF), perm=INWARD)
    gate = (near_up, near_down)
    own_up_term = after(term(1, own_id), *gate)
    own_down_term = after(term(-1, own_id), *gate)
    pair_term = after(term(0, pair_id), *gate)
    own_term = after(term(0, own_id), *gate)
    own_up = send(upper(own_up_term, own_top), perm=UP)
    own_down = send(lower(own_down_term, own_bottom), perm=DOWN)
    pair_in = send(plus(pair_term, pair_up, pair_down, far_mid).astype(BF), perm=SWAP)
    near_mid = send(plus(near_sum, near_in).astype(BF), perm=MIDDLE)
    gradient = plus(own_term, own_up, own_down, near_mid, pair_in)

    moment_one = BETA_ONE * first_moment[0] + (1.0 - BETA_ONE) * gradient
    moment_two = BETA_TWO * second_moment[0] + (1.0 - BETA_TWO) * gradient * gradient
    update_delta = (
        LEARN_RATE * (moment_one / (jnp.sqrt(moment_two) + ADAM_EPS) + DECAY * local_weight)
        - drift_local
    )
    codes = update_delta.astype(BF)
    mean_delta = reduce_rep(codes) / F32(lax.axis_size("rep"))
    return outer_step(mean_delta, momentum, base_weight)


def solution(mesh):
    placed = (
        P("rep", "fsdp", None),
        P("rep", "fsdp", None),
        P("rep", "fsdp", None),
        P("rep", "fsdp", None),
        P("rep", "fsdp", None),
        P("fsdp", None),
        P("fsdp", None),
    )
    return jax.shard_map(
        on_device,
        mesh=mesh,
        in_specs=placed,
        out_specs=(P("fsdp", None), P("fsdp", None)),
        check_vma=False,
    )
```

```python
import functools

import jax
import jax.numpy as jnp
from jax import lax
from jax.sharding import PartitionSpec as P

LEARN_RATE = 1.0
BETA_ONE = 0.9
BETA_TWO = 0.95
ADAM_EPS = 1e-08
DECAY = 0.1
OUTER_MU = 0.9
OUTER_RATE = 0.7

NY, NZ = 4, 4
BF, F32 = jnp.bfloat16, jnp.float32


def y_shift(dy):
    return [(y * NZ + z, ((y + dy) % NY) * NZ + z) for y in range(NY) for z in range(NZ)]


def z_pairs(pairs):
    return [(y * NZ + a, y * NZ + b) for y in range(NY) for a, b in pairs]


UP, DOWN = y_shift(1), y_shift(-1)
SWAP = z_pairs([(0, 1), (1, 0), (2, 3), (3, 2)])
MIDDLE = z_pairs([(1, 2), (2, 1)])
OUTWARD = z_pairs([(1, 0), (2, 3)])
CROSS_TWO = z_pairs([(z, z ^ 2) for z in range(NZ)])
CROSS_THREE = z_pairs([(z, z ^ 3) for z in range(NZ)])


def rep_shift(dx, dh, dc):
    return [
        ((x * 2 + h) * 2 + c, (((x + dx) % 4) * 2 + (h ^ dh)) * 2 + (c ^ dc))
        for x in range(4)
        for h in range(2)
        for c in range(2)
    ]


send = functools.partial(lax.ppermute, axis_name="fsdp")


def send_rep(value, dx, dh, dc):
    return lax.ppermute(value, "rep", rep_shift(dx, dh, dc))


def after(value, *earlier):
    rows = sum(array[:1].astype(F32) for array in earlier)
    return jnp.where(rows == rows, value, jnp.zeros_like(value))


def column_ids(z):
    return z, z ^ 1, jnp.where(z < 2, 2, 1), jnp.where(z < 2, 3, 0)


def reduce_rep(codes):
    rep = lax.axis_index("rep")
    x, core = rep // 4, rep % 2
    rows = codes.shape[0]
    half, piece = rows // 2, rows // 8
    mine = lax.dynamic_slice_in_dim(codes, core * half, half, 0)
    other = lax.dynamic_slice_in_dim(codes, (1 - core) * half, half, 0)
    pair = mine.astype(F32) + send_rep(other, 0, 0, 1).astype(F32)
    part = lambda d: lax.dynamic_slice_in_dim(pair, ((x + d) % 4) * piece, piece, 0)
    total = part(0)
    for d in (1, 2, 3):
        total = total + send_rep(part(d).astype(BF), d, 0, 0).astype(F32)
    rounded = total.astype(BF)
    total = rounded.astype(F32) + send_rep(rounded, 0, 1, 0).astype(F32)
    mean = (total / F32(lax.axis_size("rep"))).astype(BF)
    pieces = jnp.zeros((half, codes.shape[1]), BF)
    pieces = lax.dynamic_update_slice_in_dim(pieces, mean, x * piece, 0)
    for d in (1, 2, 3):
        pieces = lax.dynamic_update_slice_in_dim(
            pieces, send_rep(mean, d, 0, 0), ((x - d) % 4) * piece, 0
        )
    theirs = send_rep(pieces, 0, 0, 1)
    low = jnp.where(core == 0, pieces, theirs)
    high = jnp.where(core == 0, theirs, pieces)
    return jnp.concatenate([low, high], 0).astype(F32)


def outer_step(mean_delta, momentum, base_weight):
    new_momentum = OUTER_MU * momentum + mean_delta
    new_base = base_weight - OUTER_RATE * (mean_delta + OUTER_MU * new_momentum)
    return (new_base, new_momentum)


def on_device(inputs, targets, replica_drift, first_moment, second_moment, base_weight, momentum):
    tok_rows = inputs[0]
    width = tok_rows.shape[1]
    shard_rows = base_weight.shape[0]
    index = lax.axis_index("fsdp")
    y, z = index // NZ, index % NZ
    drift_local = replica_drift[0].astype(F32)
    local_weight = base_weight + drift_local
    low_weight = local_weight.astype(BF)

    def tokens(row, column, begin, size):
        start = ((y + row) % NY * NZ + column) * shard_rows + begin
        return lax.dynamic_slice_in_dim(tok_rows, start, size, 1)

    half = shard_rows // 2
    own_id, pair_id, near_id, far_id = column_ids(z)
    inner = (z == 1) | (z == 2)

    def add(total, row, column, part, begin=0):
        return total + jnp.dot(
            tokens(row, column, begin, part.shape[0]), part, preferred_element_type=F32
        )

    own = low_weight
    pair = send(own, perm=SWAP)
    near_in = send(own, perm=MIDDLE)
    own_below = send(own, perm=UP)
    own_above = send(own, perm=DOWN)
    far_in = send(pair, perm=MIDDLE)
    near_out = send(near_in, perm=OUTWARD)
    pair_below = send(pair, perm=UP)
    pair_above = send(pair, perm=DOWN)
    own_top = send(own_below[:half], perm=UP)
    own_bottom = send(own_above[half:], perm=DOWN)
    far_out = send(far_in, perm=OUTWARD)
    near = after(jnp.where(inner, near_in, near_out), pair_below, pair_above)
    near_below = send(near, perm=UP)
    near_above = send(near, perm=DOWN)

    total = jnp.dot(tokens(0, own_id, 0, shard_rows), own, preferred_element_type=F32)
    total = after(add(total, 0, pair_id, pair), near_out)
    total = add(total, -1, own_id, own_below)
    total = after(add(total, 1, own_id, own_above), near_out)

    pair_top = send(after(pair_below[:half], own_top, own_bottom), perm=UP)
    pair_bottom = send(after(pair_above[half:], own_top, own_bottom), perm=DOWN)
    far = after(jnp.where(inner, far_in, far_out), near_below, near_above, total)
    far_below = send(far, perm=UP)
    far_above = send(far, perm=DOWN)

    total = add(total, 2, own_id, own_top, 0)
    total = add(total, 2, own_id, own_bottom, half)
    total = add(total, -1, pair_id, pair_below)
    total = add(total, 1, pair_id, pair_above)
    total = add(total, 0, near_id, near)
    total = add(total, -1, near_id, near_below)
    total = add(total, 1, near_id, near_above)

    near_top = send(after(near_below[:half], pair_top, pair_bottom, total), perm=UP)
    near_bottom = send(after(near_above[half:], pair_top, pair_bottom, total), perm=DOWN)
    total = add(total, 2, pair_id, pair_top, 0)
    total = add(total, 2, pair_id, pair_bottom, half)
    total = add(total, 0, far_id, far)
    far_top = send(after(far_below[:half], total), perm=UP)
    far_bottom = send(after(far_above[half:], total), perm=DOWN)
    total = add(total, -1, far_id, far_below)
    total = add(total, 1, far_id, far_above)
    total = add(total, 2, near_id, near_top, 0)
    total = add(total, 2, near_id, near_bottom, half)
    total = add(total, 2, far_id, far_top, 0)
    total = add(total, 2, far_id, far_bottom, half)

    projected = total / jnp.sqrt(F32(width))
    residual_rows = (projected - targets[0].astype(F32)).astype(BF)
    all_tokens = tok_rows.shape[0] * lax.axis_size("fsdp")
    grad_scale = 1.0 / (jnp.sqrt(F32(width)) * F32(all_tokens))

    def term(row, column, begin=0, size=shard_rows):
        product = lax.dot_general(
            tokens(row, column, begin, size),
            residual_rows,
            (((0,), (0,)), ((), ())),
            preferred_element_type=F32,
        )
        return (product * grad_scale).astype(BF)

    def plus(first, *others):
        return sum((other.astype(F32) for other in others), first.astype(F32))

    def upper(block, top):
        return jnp.concatenate([plus(block[:half], top).astype(BF), block[half:]], 0)

    def lower(block, bottom):
        return jnp.concatenate([block[:half], plus(block[half:], bottom).astype(BF)], 0)

    near_id, far_id = z ^ 2, z ^ 3
    far_top = send(term(2, far_id, 0, half), perm=UP)
    far_bottom = send(term(2, far_id, half, half), perm=DOWN)
    near_top = send(term(2, near_id, 0, half), perm=UP)
    near_bottom = send(term(2, near_id, half, half), perm=DOWN)
    far_up = send(upper(term(1, far_id), far_top), perm=UP)
    far_down = send(lower(term(-1, far_id), far_bottom), perm=DOWN)
    gate = (far_top, far_bottom)
    near_up_term = after(term(1, near_id), *gate)
    near_down_term = after(term(-1, near_id), *gate)
    far_term = after(term(0, far_id), *gate)
    gate = (near_top, near_bottom)
    pair_top = send(after(term(2, pair_id, 0, half), *gate), perm=UP)
    pair_bottom = send(after(term(2, pair_id, half, half), *gate), perm=DOWN)
    far_in = send(plus(far_term, far_up, far_down).astype(BF), perm=CROSS_THREE)
    gate = (far_up, far_down)
    near_up = send(after(upper(near_up_term, near_top), *gate), perm=UP)
    near_down = send(after(lower(near_down_term, near_bottom), *gate), perm=DOWN)
    own_top = send(after(term(2, own_id, 0, half), *gate), perm=UP)
    own_bottom = send(after(term(2, own_id, half, half), *gate), perm=DOWN)
    near_term = after(term(0, near_id), *gate)
    pair_up_term = after(term(1, pair_id), *gate)
    pair_down_term = after(term(-1, pair_id), *gate)
    gate = (own_top, own_bottom)
    pair_up = send(after(upper(pair_up_term, pair_top), *gate), perm=UP)
    pair_down = send(after(lower(pair_down_term, pair_bottom), *gate), perm=DOWN)
    near_in = send(plus(near_term, near_up, near_down).astype(BF), perm=CROSS_TWO)
    gate = (near_up, near_down)
    own_up_term = after(term(1, own_id), *gate)
    own_down_term = after(term(-1, own_id), *gate)
    pair_term = after(term(0, pair_id), *gate)
    own_term = after(term(0, own_id), *gate)
    own_up = send(after(upper(own_up_term, own_top), pair_up, pair_down), perm=UP)
    own_down = send(after(lower(own_down_term, own_bottom), pair_up, pair_down), perm=DOWN)
    pair_in = send(plus(pair_term, pair_up, pair_down).astype(BF), perm=SWAP)
    gradient = plus(own_term, own_up, own_down, far_in, near_in, pair_in)

    moment_one = BETA_ONE * first_moment[0] + (1.0 - BETA_ONE) * gradient
    moment_two = BETA_TWO * second_moment[0] + (1.0 - BETA_TWO) * gradient * gradient
    update_delta = (
        LEARN_RATE * (moment_one / (jnp.sqrt(moment_two) + ADAM_EPS) + DECAY * local_weight)
        - drift_local
    )
    codes = update_delta.astype(BF)
    mean_delta = reduce_rep(codes)
    return outer_step(mean_delta, momentum, base_weight)


def solution(mesh):
    placed = (
        P("rep", "fsdp", None),
        P("rep", "fsdp", None),
        P("rep", "fsdp", None),
        P("rep", "fsdp", None),
        P("rep", "fsdp", None),
        P("fsdp", None),
        P("fsdp", None),
    )
    return jax.shard_map(
        on_device,
        mesh=mesh,
        in_specs=placed,
        out_specs=(P("fsdp", None), P("fsdp", None)),
        check_vma=False,
    )
```

```python
import functools

import jax
import jax.numpy as jnp
from jax import lax
from jax.sharding import PartitionSpec as P

LEARN_RATE = 1.0
BETA_ONE = 0.9
BETA_TWO = 0.95
ADAM_EPS = 1e-08
DECAY = 0.1
OUTER_MU = 0.9
OUTER_RATE = 0.7

NY, NZ = 4, 4
BF, F32 = jnp.bfloat16, jnp.float32


def y_shift(dy):
    return [(y * NZ + z, ((y + dy) % NY) * NZ + z) for y in range(NY) for z in range(NZ)]


def z_pairs(pairs):
    return [(y * NZ + a, y * NZ + b) for y in range(NY) for a, b in pairs]


UP, DOWN = y_shift(1), y_shift(-1)
SWAP = z_pairs([(0, 1), (1, 0), (2, 3), (3, 2)])
MIDDLE = z_pairs([(1, 2), (2, 1)])
OUTWARD = z_pairs([(1, 0), (2, 3)])
CROSS_TWO = z_pairs([(z, z ^ 2) for z in range(NZ)])
CROSS_THREE = z_pairs([(z, z ^ 3) for z in range(NZ)])


def rep_shift(dx, dh, dc):
    return [
        ((x * 2 + h) * 2 + c, (((x + dx) % 4) * 2 + (h ^ dh)) * 2 + (c ^ dc))
        for x in range(4)
        for h in range(2)
        for c in range(2)
    ]


send = functools.partial(lax.ppermute, axis_name="fsdp")


def send_rep(value, dx, dh, dc):
    return lax.ppermute(value, "rep", rep_shift(dx, dh, dc))


def after(value, *earlier):
    rows = sum(array[:1].astype(F32) for array in earlier)
    return jnp.where(rows == rows, value, jnp.zeros_like(value))


def column_ids(z):
    return z, z ^ 1, jnp.where(z < 2, 2, 1), jnp.where(z < 2, 3, 0)


def reduce_rep(codes):
    rep = lax.axis_index("rep")
    x, core = rep // 4, rep % 2
    rows = codes.shape[0]
    half, piece = rows // 2, rows // 8
    mine = lax.dynamic_slice_in_dim(codes, core * half, half, 0)
    other = lax.dynamic_slice_in_dim(codes, (1 - core) * half, half, 0)
    pair = mine.astype(F32) + send_rep(other, 0, 0, 1).astype(F32)
    part = lambda d: lax.dynamic_slice_in_dim(pair, ((x + d) % 4) * piece, piece, 0)
    total = part(0)
    for d in (1, 2, 3):
        total = total + send_rep(part(d).astype(BF), d, 0, 0).astype(F32)
    rounded = total.astype(BF)
    total = rounded.astype(F32) + send_rep(rounded, 0, 1, 0).astype(F32)
    mean = (total / F32(lax.axis_size("rep"))).astype(BF)
    pieces = jnp.zeros((half, codes.shape[1]), BF)
    pieces = lax.dynamic_update_slice_in_dim(pieces, mean, x * piece, 0)
    for d in (1, 2, 3):
        pieces = lax.dynamic_update_slice_in_dim(
            pieces, send_rep(mean, d, 0, 0), ((x - d) % 4) * piece, 0
        )
    theirs = send_rep(pieces, 0, 0, 1)
    low = jnp.where(core == 0, pieces, theirs)
    high = jnp.where(core == 0, theirs, pieces)
    return jnp.concatenate([low, high], 0).astype(F32)


def outer_step(mean_delta, momentum, base_weight):
    new_momentum = OUTER_MU * momentum + mean_delta
    new_base = base_weight - OUTER_RATE * (mean_delta + OUTER_MU * new_momentum)
    return (new_base, new_momentum)


def on_device(inputs, targets, replica_drift, first_moment, second_moment, base_weight, momentum):
    tok_rows = inputs[0]
    width = tok_rows.shape[1]
    shard_rows = base_weight.shape[0]
    index = lax.axis_index("fsdp")
    y, z = index // NZ, index % NZ
    drift_local = replica_drift[0].astype(F32)
    local_weight = base_weight + drift_local
    low_weight = local_weight.astype(BF)

    def tokens(row, column, begin, size):
        start = ((y + row) % NY * NZ + column) * shard_rows + begin
        return lax.dynamic_slice_in_dim(tok_rows, start, size, 1)

    half = shard_rows // 2
    own_id, pair_id, near_id, far_id = column_ids(z)
    inner = (z == 1) | (z == 2)

    def add(total, row, column, part, begin=0):
        return total + jnp.dot(
            tokens(row, column, begin, part.shape[0]), part, preferred_element_type=F32
        )

    own = low_weight
    pair = send(own, perm=SWAP)
    near_in = send(own, perm=MIDDLE)
    own_below = send(own, perm=UP)
    own_above = send(own, perm=DOWN)
    far_in = send(pair, perm=MIDDLE)
    near_out = send(near_in, perm=OUTWARD)
    pair_below = send(pair, perm=UP)
    pair_above = send(pair, perm=DOWN)
    own_top = send(own_below[:half], perm=UP)
    own_bottom = send(own_above[half:], perm=DOWN)
    far_out = send(far_in, perm=OUTWARD)
    near = after(jnp.where(inner, near_in, near_out), pair_below, pair_above)
    near_below = send(near, perm=UP)
    near_above = send(near, perm=DOWN)

    total = jnp.dot(tokens(0, own_id, 0, shard_rows), own, preferred_element_type=F32)
    total = after(add(total, 0, pair_id, pair), near_out)
    total = add(total, -1, own_id, own_below)
    total = after(add(total, 1, own_id, own_above), near_out)

    pair_top = send(after(pair_below[:half], own_top, own_bottom), perm=UP)
    pair_bottom = send(after(pair_above[half:], own_top, own_bottom), perm=DOWN)
    far = after(jnp.where(inner, far_in, far_out), near_below, near_above, total)
    far_below = send(far, perm=UP)
    far_above = send(far, perm=DOWN)

    total = add(total, 2, own_id, own_top, 0)
    total = add(total, 2, own_id, own_bottom, half)
    total = add(total, -1, pair_id, pair_below)
    total = add(total, 1, pair_id, pair_above)
    total = add(total, 0, near_id, near)
    total = add(total, -1, near_id, near_below)
    total = add(total, 1, near_id, near_above)

    near_top = send(after(near_below[:half], pair_top, pair_bottom, total), perm=UP)
    near_bottom = send(after(near_above[half:], pair_top, pair_bottom, total), perm=DOWN)
    total = add(total, 2, pair_id, pair_top, 0)
    total = add(total, 2, pair_id, pair_bottom, half)
    total = add(total, 0, far_id, far)
    far_top = send(after(far_below[:half], total), perm=UP)
    far_bottom = send(after(far_above[half:], total), perm=DOWN)
    total = add(total, -1, far_id, far_below)
    total = add(total, 1, far_id, far_above)
    total = add(total, 2, near_id, near_top, 0)
    total = add(total, 2, near_id, near_bottom, half)
    total = add(total, 2, far_id, far_top, 0)
    total = add(total, 2, far_id, far_bottom, half)

    projected = total / jnp.sqrt(F32(width))
    residual_rows = (projected - targets[0].astype(F32)).astype(BF)
    all_tokens = tok_rows.shape[0] * lax.axis_size("fsdp")
    grad_scale = 1.0 / (jnp.sqrt(F32(width)) * F32(all_tokens))

    def term(row, column, begin=0, size=shard_rows):
        product = lax.dot_general(
            tokens(row, column, begin, size),
            residual_rows,
            (((0,), (0,)), ((), ())),
            preferred_element_type=F32,
        )
        return (product * grad_scale).astype(BF)

    def plus(first, *others):
        return sum((other.astype(F32) for other in others), first.astype(F32))

    def upper(block, top):
        return jnp.concatenate([plus(block[:half], top).astype(BF), block[half:]], 0)

    def lower(block, bottom):
        return jnp.concatenate([block[:half], plus(block[half:], bottom).astype(BF)], 0)

    near_id, far_id = z ^ 2, z ^ 3
    far_top = send(term(2, far_id, 0, half), perm=UP)
    far_bottom = send(term(2, far_id, half, half), perm=DOWN)
    near_top = send(term(2, near_id, 0, half), perm=UP)
    near_bottom = send(term(2, near_id, half, half), perm=DOWN)
    far_up = send(upper(term(1, far_id), far_top), perm=UP)
    far_down = send(lower(term(-1, far_id), far_bottom), perm=DOWN)
    gate = (far_top, far_bottom)
    near_up_term = after(term(1, near_id), *gate)
    near_down_term = after(term(-1, near_id), *gate)
    far_term = after(term(0, far_id), *gate)
    gate = (near_top, near_bottom)
    pair_top = send(after(term(2, pair_id, 0, half), *gate), perm=UP)
    pair_bottom = send(after(term(2, pair_id, half, half), *gate), perm=DOWN)
    far_sum = plus(far_term, far_up, far_down).astype(BF)
    far_in = send(far_sum, perm=CROSS_THREE)
    gate = (far_up, far_down)
    near_up = send(after(upper(near_up_term, near_top), *gate), perm=UP)
    near_down = send(after(lower(near_down_term, near_bottom), *gate), perm=DOWN)
    near_term = after(term(0, near_id), *gate)
    pair_up_term = after(term(1, pair_id), *gate)
    pair_down_term = after(term(-1, pair_id), *gate)
    pair_up = send(after(upper(pair_up_term, pair_top), far_sum), perm=UP)
    pair_down = send(after(lower(pair_down_term, pair_bottom), far_sum), perm=DOWN)
    near_in = send(plus(near_term, near_up, near_down).astype(BF), perm=CROSS_TWO)
    gate = (near_up, near_down)
    own_top = send(after(term(2, own_id, 0, half), *gate), perm=UP)
    own_bottom = send(after(term(2, own_id, half, half), *gate), perm=DOWN)
    own_up_term = after(term(1, own_id), *gate)
    own_down_term = after(term(-1, own_id), *gate)
    pair_term = after(term(0, pair_id), *gate)
    own_term = after(term(0, own_id), *gate)
    own_up = send(after(upper(own_up_term, own_top), pair_up, pair_down, far_in), perm=UP)
    own_down = send(after(lower(own_down_term, own_bottom), pair_up, pair_down, far_in), perm=DOWN)
    pair_in = send(plus(pair_term, pair_up, pair_down).astype(BF), perm=SWAP)
    gradient = plus(own_term, own_up, own_down, far_in, near_in, pair_in)

    moment_one = BETA_ONE * first_moment[0] + (1.0 - BETA_ONE) * gradient
    moment_two = BETA_TWO * second_moment[0] + (1.0 - BETA_TWO) * gradient * gradient
    update_delta = (
        LEARN_RATE * (moment_one / (jnp.sqrt(moment_two) + ADAM_EPS) + DECAY * local_weight)
        - drift_local
    )
    codes = update_delta.astype(BF)
    mean_delta = reduce_rep(codes)
    return outer_step(mean_delta, momentum, base_weight)


def solution(mesh):
    placed = (
        P("rep", "fsdp", None),
        P("rep", "fsdp", None),
        P("rep", "fsdp", None),
        P("rep", "fsdp", None),
        P("rep", "fsdp", None),
        P("fsdp", None),
        P("fsdp", None),
    )
    return jax.shard_map(
        on_device,
        mesh=mesh,
        in_specs=placed,
        out_specs=(P("fsdp", None), P("fsdp", None)),
        check_vma=False,
    )
```

```python
import functools

import jax
import jax.numpy as jnp
from jax import lax
from jax.sharding import PartitionSpec as P

LEARN_RATE = 1.0
BETA_ONE = 0.9
BETA_TWO = 0.95
ADAM_EPS = 1e-08
DECAY = 0.1
OUTER_MU = 0.9
OUTER_RATE = 0.7

NY, NZ = 4, 4
BF, F32 = jnp.bfloat16, jnp.float32


def y_shift(dy):
    return [(y * NZ + z, ((y + dy) % NY) * NZ + z) for y in range(NY) for z in range(NZ)]


def z_pairs(pairs):
    return [(y * NZ + a, y * NZ + b) for y in range(NY) for a, b in pairs]


UP, DOWN = y_shift(1), y_shift(-1)
SWAP = z_pairs([(0, 1), (1, 0), (2, 3), (3, 2)])
MIDDLE = z_pairs([(1, 2), (2, 1)])
OUTWARD = z_pairs([(1, 0), (2, 3)])
CROSS_TWO = z_pairs([(z, z ^ 2) for z in range(NZ)])
CROSS_THREE = z_pairs([(z, z ^ 3) for z in range(NZ)])


def rep_shift(dx, dh, dc):
    return [
        ((x * 2 + h) * 2 + c, (((x + dx) % 4) * 2 + (h ^ dh)) * 2 + (c ^ dc))
        for x in range(4)
        for h in range(2)
        for c in range(2)
    ]


send = functools.partial(lax.ppermute, axis_name="fsdp")


def send_rep(value, dx, dh, dc):
    return lax.ppermute(value, "rep", rep_shift(dx, dh, dc))


def after(value, *earlier):
    rows = sum(array[:1].astype(F32) for array in earlier)
    return jnp.where(rows == rows, value, jnp.zeros_like(value))


def column_ids(z):
    return z, z ^ 1, jnp.where(z < 2, 2, 1), jnp.where(z < 2, 3, 0)


def reduce_rep(codes):
    rep = lax.axis_index("rep")
    x, core = rep // 4, rep % 2
    rows = codes.shape[0]
    half, piece = rows // 2, rows // 8
    mine = lax.dynamic_slice_in_dim(codes, core * half, half, 0)
    other = lax.dynamic_slice_in_dim(codes, (1 - core) * half, half, 0)
    pair = mine.astype(F32) + send_rep(other, 0, 0, 1).astype(F32)
    part = lambda d: lax.dynamic_slice_in_dim(pair, ((x + d) % 4) * piece, piece, 0)
    total = part(0)
    for d in (1, 2, 3):
        total = total + send_rep(part(d).astype(BF), d, 0, 0).astype(F32)
    rounded = total.astype(BF)
    total = rounded.astype(F32) + send_rep(rounded, 0, 1, 0).astype(F32)
    mean = (total / F32(lax.axis_size("rep"))).astype(BF)
    pieces = jnp.zeros((half, codes.shape[1]), BF)
    pieces = lax.dynamic_update_slice_in_dim(pieces, mean, x * piece, 0)
    for d in (1, 2, 3):
        pieces = lax.dynamic_update_slice_in_dim(
            pieces, send_rep(mean, d, 0, 0), ((x - d) % 4) * piece, 0
        )
    theirs = send_rep(pieces, 0, 0, 1)
    low = jnp.where(core == 0, pieces, theirs)
    high = jnp.where(core == 0, theirs, pieces)
    return jnp.concatenate([low, high], 0).astype(F32)


def outer_step(mean_delta, momentum, base_weight):
    new_momentum = OUTER_MU * momentum + mean_delta
    new_base = base_weight - OUTER_RATE * (mean_delta + OUTER_MU * new_momentum)
    return (new_base, new_momentum)


def on_device(inputs, targets, replica_drift, first_moment, second_moment, base_weight, momentum):
    tok_rows = inputs[0]
    width = tok_rows.shape[1]
    shard_rows = base_weight.shape[0]
    index = lax.axis_index("fsdp")
    y, z = index // NZ, index % NZ
    drift_local = replica_drift[0].astype(F32)
    local_weight = base_weight + drift_local
    low_weight = local_weight.astype(BF)

    def tokens(row, column, begin, size):
        start = ((y + row) % NY * NZ + column) * shard_rows + begin
        return lax.dynamic_slice_in_dim(tok_rows, start, size, 1)

    half = shard_rows // 2
    own_id, pair_id, near_id, far_id = column_ids(z)
    inner = (z == 1) | (z == 2)

    def add(total, row, column, part, begin=0):
        return total + jnp.dot(
            tokens(row, column, begin, part.shape[0]), part, preferred_element_type=F32
        )

    own = low_weight
    pair = send(own, perm=SWAP)
    near_in = send(own, perm=MIDDLE)
    own_below = send(own, perm=UP)
    own_above = send(own, perm=DOWN)
    far_in = send(pair, perm=MIDDLE)
    near_out = send(near_in, perm=OUTWARD)
    pair_below = send(pair, perm=UP)
    pair_above = send(pair, perm=DOWN)
    own_top = send(own_below[:half], perm=UP)
    own_bottom = send(own_above[half:], perm=DOWN)
    far_out = send(far_in, perm=OUTWARD)
    near = after(jnp.where(inner, near_in, near_out), own_top, own_bottom)
    near_below = send(near, perm=UP)
    near_above = send(near, perm=DOWN)

    total = jnp.dot(tokens(0, own_id, 0, shard_rows), own, preferred_element_type=F32)
    total = after(add(total, 0, pair_id, pair), near_out)
    total = add(total, -1, own_id, own_below)
    total = after(add(total, 1, own_id, own_above), near_out)

    pair_top = send(after(pair_below[:half], own_top, own_bottom), perm=UP)
    pair_bottom = send(after(pair_above[half:], own_top, own_bottom), perm=DOWN)
    far = after(jnp.where(inner, far_in, far_out), near_below, near_above, total)
    far_below = send(far, perm=UP)
    far_above = send(far, perm=DOWN)

    total = add(total, 2, own_id, own_top, 0)
    total = add(total, 2, own_id, own_bottom, half)
    total = add(total, -1, pair_id, pair_below)
    total = add(total, 1, pair_id, pair_above)
    total = add(total, 0, near_id, near)
    total = add(total, -1, near_id, near_below)
    total = add(total, 1, near_id, near_above)

    near_top = send(after(near_below[:half], pair_top, pair_bottom, total), perm=UP)
    near_bottom = send(after(near_above[half:], pair_top, pair_bottom, total), perm=DOWN)
    total = add(total, 2, pair_id, pair_top, 0)
    total = add(total, 2, pair_id, pair_bottom, half)
    total = add(total, 0, far_id, far)
    far_top = send(after(far_below[:half], total), perm=UP)
    far_bottom = send(after(far_above[half:], total), perm=DOWN)
    total = add(total, -1, far_id, far_below)
    total = add(total, 1, far_id, far_above)
    total = add(total, 2, near_id, near_top, 0)
    total = add(total, 2, near_id, near_bottom, half)
    total = add(total, 2, far_id, far_top, 0)
    total = add(total, 2, far_id, far_bottom, half)

    projected = total / jnp.sqrt(F32(width))
    residual_rows = (projected - targets[0].astype(F32)).astype(BF)
    all_tokens = tok_rows.shape[0] * lax.axis_size("fsdp")
    grad_scale = 1.0 / (jnp.sqrt(F32(width)) * F32(all_tokens))

    def term(row, column, begin=0, size=shard_rows):
        product = lax.dot_general(
            tokens(row, column, begin, size),
            residual_rows,
            (((0,), (0,)), ((), ())),
            preferred_element_type=F32,
        )
        return (product * grad_scale).astype(BF)

    def plus(first, *others):
        return sum((other.astype(F32) for other in others), first.astype(F32))

    def upper(block, top):
        return jnp.concatenate([plus(block[:half], top).astype(BF), block[half:]], 0)

    def lower(block, bottom):
        return jnp.concatenate([block[:half], plus(block[half:], bottom).astype(BF)], 0)

    near_id, far_id = z ^ 2, z ^ 3
    far_top = send(term(2, far_id, 0, half), perm=UP)
    far_bottom = send(term(2, far_id, half, half), perm=DOWN)
    near_top = send(term(2, near_id, 0, half), perm=UP)
    near_bottom = send(term(2, near_id, half, half), perm=DOWN)
    far_up = send(upper(term(1, far_id), far_top), perm=UP)
    far_down = send(lower(term(-1, far_id), far_bottom), perm=DOWN)
    gate = (far_top, far_bottom)
    near_up_term = after(term(1, near_id), *gate)
    near_down_term = after(term(-1, near_id), *gate)
    far_term = after(term(0, far_id), *gate)
    gate = (near_top, near_bottom)
    pair_top = send(after(term(2, pair_id, 0, half), *gate), perm=UP)
    pair_bottom = send(after(term(2, pair_id, half, half), *gate), perm=DOWN)
    far_sum = plus(far_term, far_up, far_down).astype(BF)
    far_in = send(far_sum, perm=CROSS_THREE)
    gate = (far_up, far_down)
    near_up = send(after(upper(near_up_term, near_top), *gate), perm=UP)
    near_down = send(after(lower(near_down_term, near_bottom), *gate), perm=DOWN)
    near_term = after(term(0, near_id), *gate)
    pair_up_term = after(term(1, pair_id), *gate)
    pair_down_term = after(term(-1, pair_id), *gate)
    pair_up = send(after(upper(pair_up_term, pair_top), far_sum), perm=UP)
    pair_down = send(after(lower(pair_down_term, pair_bottom), far_sum), perm=DOWN)
    near_in = send(plus(near_term, near_up, near_down).astype(BF), perm=CROSS_TWO)
    gate = (near_up, near_down)
    own_top = send(after(term(2, own_id, 0, half), *gate), perm=UP)
    own_bottom = send(after(term(2, own_id, half, half), *gate), perm=DOWN)
    own_up_term = after(term(1, own_id), *gate)
    own_down_term = after(term(-1, own_id), *gate)
    pair_term = after(term(0, pair_id), *gate)
    own_term = after(term(0, own_id), *gate)
    own_up = send(after(upper(own_up_term, own_top), pair_up, pair_down, far_in), perm=UP)
    own_down = send(after(lower(own_down_term, own_bottom), pair_up, pair_down, far_in), perm=DOWN)
    pair_in = send(plus(pair_term, pair_up, pair_down).astype(BF), perm=SWAP)
    gradient = plus(own_term, own_up, own_down, far_in, near_in, pair_in)

    moment_one = BETA_ONE * first_moment[0] + (1.0 - BETA_ONE) * gradient
    moment_two = BETA_TWO * second_moment[0] + (1.0 - BETA_TWO) * gradient * gradient
    update_delta = (
        LEARN_RATE * (moment_one / (jnp.sqrt(moment_two) + ADAM_EPS) + DECAY * local_weight)
        - drift_local
    )
    codes = update_delta.astype(BF)
    mean_delta = reduce_rep(codes)
    return outer_step(mean_delta, momentum, base_weight)


def solution(mesh):
    placed = (
        P("rep", "fsdp", None),
        P("rep", "fsdp", None),
        P("rep", "fsdp", None),
        P("rep", "fsdp", None),
        P("rep", "fsdp", None),
        P("fsdp", None),
        P("fsdp", None),
    )
    return jax.shard_map(
        on_device,
        mesh=mesh,
        in_specs=placed,
        out_specs=(P("fsdp", None), P("fsdp", None)),
        check_vma=False,
    )
```

```python
import functools

import jax
import jax.numpy as jnp
from jax import lax
from jax.sharding import PartitionSpec as P

LEARN_RATE = 1.0
BETA_ONE = 0.9
BETA_TWO = 0.95
ADAM_EPS = 1e-08
DECAY = 0.1
OUTER_MU = 0.9
OUTER_RATE = 0.7

NY, NZ = 4, 4
BF, F32 = jnp.bfloat16, jnp.float32


def y_shift(dy):
    return [(y * NZ + z, ((y + dy) % NY) * NZ + z) for y in range(NY) for z in range(NZ)]


def z_pairs(pairs):
    return [(y * NZ + a, y * NZ + b) for y in range(NY) for a, b in pairs]


UP, DOWN = y_shift(1), y_shift(-1)
SWAP = z_pairs([(0, 1), (1, 0), (2, 3), (3, 2)])
MIDDLE = z_pairs([(1, 2), (2, 1)])
OUTWARD = z_pairs([(1, 0), (2, 3)])
CROSS_TWO = z_pairs([(z, z ^ 2) for z in range(NZ)])
CROSS_THREE = z_pairs([(z, z ^ 3) for z in range(NZ)])


def rep_shift(dx, dh, dc):
    return [
        ((x * 2 + h) * 2 + c, (((x + dx) % 4) * 2 + (h ^ dh)) * 2 + (c ^ dc))
        for x in range(4)
        for h in range(2)
        for c in range(2)
    ]


send = functools.partial(lax.ppermute, axis_name="fsdp")


def send_rep(value, dx, dh, dc):
    return lax.ppermute(value, "rep", rep_shift(dx, dh, dc))


def after(value, *earlier):
    rows = sum(array[:1].astype(F32) for array in earlier)
    return jnp.where(rows == rows, value, jnp.zeros_like(value))


def column_ids(z):
    return z, z ^ 1, jnp.where(z < 2, 2, 1), jnp.where(z < 2, 3, 0)


def reduce_rep(codes):
    rep = lax.axis_index("rep")
    x, core = rep // 4, rep % 2
    rows = codes.shape[0]
    half, piece = rows // 2, rows // 8
    mine = lax.dynamic_slice_in_dim(codes, core * half, half, 0)
    other = lax.dynamic_slice_in_dim(codes, (1 - core) * half, half, 0)
    pair = mine.astype(F32) + send_rep(other, 0, 0, 1).astype(F32)
    part = lambda d: lax.dynamic_slice_in_dim(pair, ((x + d) % 4) * piece, piece, 0)
    total = part(0)
    for d in (1, 2, 3):
        total = total + send_rep(part(d).astype(BF), d, 0, 0).astype(F32)
    rounded = total.astype(BF)
    total = rounded.astype(F32) + send_rep(rounded, 0, 1, 0).astype(F32)
    mean = (total / F32(lax.axis_size("rep"))).astype(BF)
    pieces = jnp.zeros((half, codes.shape[1]), BF)
    pieces = lax.dynamic_update_slice_in_dim(pieces, mean, x * piece, 0)
    for d in (1, 2, 3):
        pieces = lax.dynamic_update_slice_in_dim(
            pieces, send_rep(mean, d, 0, 0), ((x - d) % 4) * piece, 0
        )
    theirs = send_rep(pieces, 0, 0, 1)
    low = jnp.where(core == 0, pieces, theirs)
    high = jnp.where(core == 0, theirs, pieces)
    return jnp.concatenate([low, high], 0).astype(F32)


def outer_step(mean_delta, momentum, base_weight):
    new_momentum = OUTER_MU * momentum + mean_delta
    new_base = base_weight - OUTER_RATE * (mean_delta + OUTER_MU * new_momentum)
    return (new_base, new_momentum)


def on_device(inputs, targets, replica_drift, first_moment, second_moment, base_weight, momentum):
    tok_rows = inputs[0]
    width = tok_rows.shape[1]
    shard_rows = base_weight.shape[0]
    index = lax.axis_index("fsdp")
    y, z = index // NZ, index % NZ
    drift_local = replica_drift[0].astype(F32)
    local_weight = base_weight + drift_local
    low_weight = local_weight.astype(BF)

    def tokens(row, column, begin, size):
        start = ((y + row) % NY * NZ + column) * shard_rows + begin
        return lax.dynamic_slice_in_dim(tok_rows, start, size, 1)

    half = shard_rows // 2
    own_id, pair_id, near_id, far_id = column_ids(z)
    inner = (z == 1) | (z == 2)

    def add(total, row, column, part, begin=0):
        return total + jnp.dot(
            tokens(row, column, begin, part.shape[0]), part, preferred_element_type=F32
        )

    own = low_weight
    pair = send(own, perm=SWAP)
    near_in = send(own, perm=MIDDLE)
    own_below = send(own, perm=UP)
    own_above = send(own, perm=DOWN)
    far_in = send(pair, perm=MIDDLE)
    near_out = send(near_in, perm=OUTWARD)
    pair_below = send(pair, perm=UP)
    pair_above = send(pair, perm=DOWN)
    own_top = send(own_below[:half], perm=UP)
    own_bottom = send(own_above[half:], perm=DOWN)
    far_out = send(far_in, perm=OUTWARD)
    near = after(jnp.where(inner, near_in, near_out), own_top, own_bottom)
    near_below = send(near, perm=UP)
    near_above = send(near, perm=DOWN)

    total = jnp.dot(tokens(0, own_id, 0, shard_rows), own, preferred_element_type=F32)
    total = after(add(total, 0, pair_id, pair), near_out)
    total = add(total, -1, own_id, own_below)
    total = after(add(total, 1, own_id, own_above), near_out)

    pair_top = send(after(pair_below[:half], own_top, own_bottom), perm=UP)
    pair_bottom = send(after(pair_above[half:], own_top, own_bottom), perm=DOWN)
    far = after(jnp.where(inner, far_in, far_out), total)
    far_below = send(far, perm=UP)
    far_above = send(far, perm=DOWN)

    total = add(total, 2, own_id, own_top, 0)
    total = add(total, 2, own_id, own_bottom, half)
    total = add(total, -1, pair_id, pair_below)
    total = add(total, 1, pair_id, pair_above)
    total = add(total, 0, near_id, near)
    total = add(total, -1, near_id, near_below)
    total = add(total, 1, near_id, near_above)

    near_top = send(after(near_below[:half], pair_top, pair_bottom, total), perm=UP)
    near_bottom = send(after(near_above[half:], pair_top, pair_bottom, total), perm=DOWN)
    total = add(total, 2, pair_id, pair_top, 0)
    total = add(total, 2, pair_id, pair_bottom, half)
    total = add(total, 0, far_id, far)
    far_top = send(after(far_below[:half], total), perm=UP)
    far_bottom = send(after(far_above[half:], total), perm=DOWN)
    total = add(total, -1, far_id, far_below)
    total = add(total, 1, far_id, far_above)
    total = add(total, 2, near_id, near_top, 0)
    total = add(total, 2, near_id, near_bottom, half)
    total = add(total, 2, far_id, far_top, 0)
    total = add(total, 2, far_id, far_bottom, half)

    projected = total / jnp.sqrt(F32(width))
    residual_rows = (projected - targets[0].astype(F32)).astype(BF)
    all_tokens = tok_rows.shape[0] * lax.axis_size("fsdp")
    grad_scale = 1.0 / (jnp.sqrt(F32(width)) * F32(all_tokens))

    def term(row, column, begin=0, size=shard_rows):
        product = lax.dot_general(
            tokens(row, column, begin, size),
            residual_rows,
            (((0,), (0,)), ((), ())),
            preferred_element_type=F32,
        )
        return (product * grad_scale).astype(BF)

    def plus(first, *others):
        return sum((other.astype(F32) for other in others), first.astype(F32))

    def upper(block, top):
        return jnp.concatenate([plus(block[:half], top).astype(BF), block[half:]], 0)

    def lower(block, bottom):
        return jnp.concatenate([block[:half], plus(block[half:], bottom).astype(BF)], 0)

    near_id, far_id = z ^ 2, z ^ 3
    far_top = send(term(2, far_id, 0, half), perm=UP)
    far_bottom = send(term(2, far_id, half, half), perm=DOWN)
    near_top = send(term(2, near_id, 0, half), perm=UP)
    near_bottom = send(term(2, near_id, half, half), perm=DOWN)
    far_up = send(upper(term(1, far_id), far_top), perm=UP)
    far_down = send(lower(term(-1, far_id), far_bottom), perm=DOWN)
    gate = (far_top, far_bottom)
    near_up_term = after(term(1, near_id), *gate)
    near_down_term = after(term(-1, near_id), *gate)
    far_term = after(term(0, far_id), *gate)
    gate = (near_top, near_bottom)
    pair_top = send(after(term(2, pair_id, 0, half), *gate), perm=UP)
    pair_bottom = send(after(term(2, pair_id, half, half), *gate), perm=DOWN)
    far_sum = plus(far_term, far_up, far_down).astype(BF)
    far_in = send(far_sum, perm=CROSS_THREE)
    gate = (far_up, far_down)
    near_up = send(after(upper(near_up_term, near_top), *gate), perm=UP)
    near_down = send(after(lower(near_down_term, near_bottom), *gate), perm=DOWN)
    near_term = after(term(0, near_id), *gate)
    pair_up_term = after(term(1, pair_id), *gate)
    pair_down_term = after(term(-1, pair_id), *gate)
    pair_up = send(after(upper(pair_up_term, pair_top), far_sum), perm=UP)
    pair_down = send(after(lower(pair_down_term, pair_bottom), far_sum), perm=DOWN)
    near_in = send(plus(near_term, near_up, near_down).astype(BF), perm=CROSS_TWO)
    gate = (near_up, near_down)
    own_top = send(after(term(2, own_id, 0, half), *gate), perm=UP)
    own_bottom = send(after(term(2, own_id, half, half), *gate), perm=DOWN)
    own_up_term = after(term(1, own_id), *gate)
    own_down_term = after(term(-1, own_id), *gate)
    pair_term = after(term(0, pair_id), *gate)
    own_term = after(term(0, own_id), *gate)
    own_up = send(after(upper(own_up_term, own_top), pair_up, pair_down, far_in), perm=UP)
    own_down = send(after(lower(own_down_term, own_bottom), pair_up, pair_down, far_in), perm=DOWN)
    pair_in = send(plus(pair_term, pair_up, pair_down).astype(BF), perm=SWAP)
    gradient = plus(own_term, own_up, own_down, far_in, near_in, pair_in)

    moment_one = BETA_ONE * first_moment[0] + (1.0 - BETA_ONE) * gradient
    moment_two = BETA_TWO * second_moment[0] + (1.0 - BETA_TWO) * gradient * gradient
    update_delta = (
        LEARN_RATE * (moment_one / (jnp.sqrt(moment_two) + ADAM_EPS) + DECAY * local_weight)
        - drift_local
    )
    codes = update_delta.astype(BF)
    mean_delta = reduce_rep(codes)
    return outer_step(mean_delta, momentum, base_weight)


def solution(mesh):
    placed = (
        P("rep", "fsdp", None),
        P("rep", "fsdp", None),
        P("rep", "fsdp", None),
        P("rep", "fsdp", None),
        P("rep", "fsdp", None),
        P("fsdp", None),
        P("fsdp", None),
    )
    return jax.shard_map(
        on_device,
        mesh=mesh,
        in_specs=placed,
        out_specs=(P("fsdp", None), P("fsdp", None)),
        check_vma=False,
    )
```
